512 devices in a mesh: pool: 128 (over z, y, core), tp: 4 (over x).
Axes of the slice: x: 4, y: 4, z: 16, core: 2. Of those that a mesh axis runs over, the one named last changes fastest.
Arguments:
- queries: bfloat16 [16384, 64, 128], P(('pool', 'tp')), may hold values from -6 to 6
- fresh_key_values: bfloat16 [16384, 4, 2, 128], P(('pool', 'tp')), may hold values from -5 to 5
- pooled_page_cache: bfloat16 [5, 128, 8, 4, 2, 128], P(None, 'pool', None, 'tp'), may hold values from -5 to 5
- leaf_cache: bfloat16 [128, 256, 4, 2, 128], P('pool', None, 'tp'), may hold values from -5 to 5
- parent: int32 [133], replicated, may hold values from 0 to 4, as said below
- node_pages: int32 [5], replicated, may hold values from 64 to 128
- node_owner: int32 [5], replicated, may hold values from 0 to 127
- leaf_len: int32 [128], P('pool'), may hold values from 1 to 32
Outputs:
- attended: bfloat16 [16384, 64, 128], P(('pool', 'tp'))
The draws below stay inside these ranges and needn't reach their ends.
Inputs may be any that keep to these rules, and one draw needn't show every extreme that they name: Nodes 0 to 4 have parent 0; node 5 + r is request r's own node and its parent is one of nodes 1 to 4.
All inputs are finite; a program needn't handle non-finite values.
Results may differ from the reference program's by a relative error of at most 0.008.
Values may be sent and summed in bfloat16 or wider, within the bound.
A program may use at most 64 MiB of HBM per device.

```python
import jax
import jax.numpy as jnp
from jax import lax

QUERY_HEADS = 64
KEY_VALUE_HEADS = 4
HEAD_SIZE = 128
REQUEST_TOKENS = 128
PAGE_TOKENS = 8
LEAF_PAGES = 32
MIDS = 4
LEAF_SLOTS = 256
SHARED_NODES = 5
REQUEST_COUNT = 128
TOKEN_COUNT = 16384
N_POOL = 128


def draw_queries(key, part):
    key = jax.random.fold_in(key, 11)
    values_drawn = jnp.clip(jax.random.normal(key, (TOKEN_COUNT, QUERY_HEADS, HEAD_SIZE), jnp.float32), -5.0, 5.0)
    return values_drawn.astype(jnp.bfloat16)


def draw_leaf_cache(key, part):
    key = jax.random.fold_in(key, 13)
    array_shape = (REQUEST_COUNT, LEAF_SLOTS, KEY_VALUE_HEADS, 2, HEAD_SIZE)
    values_drawn = jnp.clip(jax.random.normal(key, array_shape, jnp.float32), -5.0, 5.0)
    return values_drawn.astype(jnp.bfloat16)


def draw_parent(key, part):
    key = jax.random.fold_in(key, 17)
    upper = jnp.zeros((1 + MIDS,), jnp.int32)
    lower = jax.random.randint(key, (REQUEST_COUNT,), 1, MIDS + 1).astype(jnp.int32)
    forced = jax.random.randint(jax.random.fold_in(key, 1), (), 0, REQUEST_COUNT)
    lower = lower.at[forced].set(MIDS)
    return jnp.concatenate([upper, lower], 0)


def draw_node_pages(key, part):
    key = jax.random.fold_in(key, 19)
    counts = jax.random.randint(key, (SHARED_NODES,), N_POOL // 2, N_POOL + 1).astype(jnp.int32)
    picked = jax.random.permutation(jax.random.fold_in(key, 1), SHARED_NODES)
    counts = counts.at[picked[0]].set(N_POOL)
    counts = counts.at[picked[1]].set(N_POOL // 2)
    return counts


def draw_leaf_len(key, part):
    key = jax.random.fold_in(key, 23)
    counts = jax.random.randint(key, (REQUEST_COUNT,), 1, LEAF_PAGES + 1).astype(jnp.int32)
    forced = jax.random.randint(jax.random.fold_in(key, 1), (), 0, REQUEST_COUNT)
    return counts.at[forced].set(LEAF_PAGES)


def touch_ends(entries, own_key, smallest, largest):
    place = [jax.random.randint(jax.random.fold_in(own_key, axis), (), 0, length) for axis, length in enumerate(entries.shape)]
    longest = entries.shape.index(max(entries.shape))
    next_to = place[:longest] + [(place[longest] + 1) % entries.shape[longest]] + place[longest + 1:]
    return entries.at[tuple(place)].set(smallest).at[tuple(next_to)].set(largest)


def level_of(own_key, dims, shards, least, high):
    loudness = 1.0
    for position, blocks in shards:
        heights = jax.random.uniform(jax.random.fold_in(jax.random.fold_in(own_key, 6), position), (blocks,), jnp.float32, least / len(shards), high / len(shards))
        loudness = loudness * jnp.repeat(jnp.exp(heights), dims[position] // blocks).reshape((-1,) + (1,) * (len(dims) - 1 - position))
    return loudness


def bell_draw(rng, extent, deviation, bound, shards=(), held_as=jnp.bfloat16):
    gain = level_of(rng, extent, shards, -0.22, 0.18) if shards else 1.0
    values = jax.random.normal(rng, extent, jnp.float32) * deviation * gain
    return jnp.minimum(jnp.maximum(values, -bound), bound).astype(held_as)


def setup_inputs(seed: int = 0) -> dict:
    key_list = jax.random.split(jax.random.key(seed), 9)
    queries = draw_queries(jax.random.fold_in(key_list[8], 71), 0)
    fresh_key_values = bell_draw(key_list[1], (TOKEN_COUNT, KEY_VALUE_HEADS, 2, HEAD_SIZE), 1.0, 5.0, ((0, 512),))
    pooled_page_cache = bell_draw(key_list[2], (SHARED_NODES, N_POOL, PAGE_TOKENS, KEY_VALUE_HEADS, 2, HEAD_SIZE), 1.0, 5.0, ((1, 128), (3, 4)))
    leaf_cache = draw_leaf_cache(jax.random.fold_in(key_list[8], 71), 0)
    parent = draw_parent(jax.random.fold_in(key_list[8], 71), 0)
    node_pages = draw_node_pages(jax.random.fold_in(key_list[8], 71), 0)
    node_owner = touch_ends(jax.random.randint(key_list[6], (SHARED_NODES,), 0, N_POOL), jax.random.fold_in(key_list[6], 1), 0, N_POOL - 1).astype(jnp.int32)
    leaf_len = draw_leaf_len(jax.random.fold_in(key_list[8], 71), 0)
    return {"queries": queries, "fresh_key_values": fresh_key_values, "pooled_page_cache": pooled_page_cache, "leaf_cache": leaf_cache, "parent": parent, "node_pages": node_pages, "node_owner": node_owner, "leaf_len": leaf_len}


def stripe_valid(page_count, owner_slot):
    slot_ids = jnp.arange(N_POOL, dtype=jnp.int32)
    usable = jnp.mod(slot_ids - owner_slot, N_POOL) < page_count
    return jnp.repeat(usable, PAGE_TOKENS)

def reference(queries, fresh_key_values, pooled_page_cache, leaf_cache, parent, node_pages, node_owner, leaf_len):
    query_group_width = QUERY_HEADS // KEY_VALUE_HEADS
    inv_root = 1.0 / jnp.sqrt(jnp.float32(HEAD_SIZE))

    def per_request(request):
        request = request.astype(jnp.int32)
        first_row = (request * REQUEST_TOKENS).astype(jnp.int32)
        query_matrix = lax.dynamic_slice_in_dim(queries, first_row, REQUEST_TOKENS, 0)
        query_matrix = query_matrix.astype(jnp.float32).reshape(REQUEST_TOKENS, KEY_VALUE_HEADS, query_group_width, HEAD_SIZE)
        mid_node = parent[1 + MIDS + request]
        root_key_values = pooled_page_cache[0].reshape(N_POOL * PAGE_TOKENS, KEY_VALUE_HEADS, 2, HEAD_SIZE)
        middle_key_values = lax.dynamic_index_in_dim(pooled_page_cache, mid_node, 0, keepdims=False)
        middle_key_values = middle_key_values.reshape(N_POOL * PAGE_TOKENS, KEY_VALUE_HEADS, 2, HEAD_SIZE)
        leaf_pairs = lax.dynamic_index_in_dim(leaf_cache, request, 0, keepdims=False)
        suffix_pairs = lax.dynamic_slice_in_dim(fresh_key_values, first_row, REQUEST_TOKENS, 0)
        key_pairs = jnp.concatenate([root_key_values, middle_key_values, leaf_pairs, suffix_pairs], 0).astype(jnp.float32)
        root_mask = stripe_valid(node_pages[0], node_owner[0])
        mid_mask = stripe_valid(node_pages[mid_node], node_owner[mid_node])
        leaf_mask = jnp.arange(LEAF_SLOTS, dtype=jnp.int32) < leaf_len[request] * PAGE_TOKENS
        row_ids = jnp.arange(REQUEST_TOKENS, dtype=jnp.int32)
        causal = row_ids[None, :] <= row_ids[:, None]
        prefix_mask = jnp.concatenate([root_mask, mid_mask, leaf_mask], 0)
        key_mask = jnp.concatenate([jnp.broadcast_to(prefix_mask[None, :], (REQUEST_TOKENS, prefix_mask.shape[0])), causal], 1)
        scores = jnp.einsum('tkgd,skd->tkgs', query_matrix, key_pairs[:, :, 0, :]) * inv_root
        wide_mask = key_mask[:, None, None, :]
        scores = jnp.where(wide_mask, scores, jnp.float32(-1e+30))
        row_max = lax.optimization_barrier(jnp.max(scores, axis=-1, keepdims=True))
        weights = jnp.where(wide_mask, jnp.exp(scores - row_max), jnp.float32(0.0))
        totals = lax.optimization_barrier(jnp.sum(weights, axis=-1))
        rounded = lax.optimization_barrier(weights.astype(jnp.bfloat16)).astype(jnp.float32)
        attended = jnp.einsum('tkgs,skd->tkgd', rounded, key_pairs[:, :, 1, :]) / totals[..., None]
        return attended.astype(jnp.bfloat16).reshape(REQUEST_TOKENS, QUERY_HEADS, HEAD_SIZE)
    everything = lax.map(per_request, jnp.arange(REQUEST_COUNT, dtype=jnp.int32))
    return everything.reshape(TOKEN_COUNT, QUERY_HEADS, HEAD_SIZE)
```

```python
import jax
import jax.numpy as jnp
from jax import lax
from jax.experimental import pallas as pl
from jax.experimental.pallas import tpu as pltpu
from jax.sharding import PartitionSpec as P

MESH = pl.DeviceIdType.MESH
BF, F32, I32 = jnp.bfloat16, jnp.float32, jnp.int32
NEG = -1e30

REL = (0, 1, -1, 2, -2, 5, -5, 4, 6, 3, 7, -4, -6, -3, -7, 8)
EARLY, LATE = (0, 7), (7, 16)
GROUPS = ((0, 1), (1, 5), (5, 7), (7, 16))


def dot_t(a, b):
    return lax.dot_general(a, b, (((1,), (1,)), ((), ())), preferred_element_type=F32)


def kernel(
    parent, pages, owners, leaf_len, queries, fresh, pooled, leaf, out,
    q_all, k1, v1, k2, v2, k3, v3, b1, b2, b3, wide, fresh_out,
    z_own, z_near, z_far, z_rest, to_y, held, other, m_ref, acc, o_all,
    zs, zr, ys, yr, cs, cr, qs, qr, fs, fr, os, orr, local,
):
    pool, x = lax.axis_index("pool"), lax.axis_index("tp")
    z, y, c = pool // 8, (pool // 2) % 4, pool % 2

    def at(dz=0, dy=0, dc=0, dx=0):
        place = ((z + dz + 16) % 16) * 8 + ((y + dy) % 4) * 2 + (c + dc) % 2
        return (place, (x + dx) % 4)

    peers = [at(dx=1), at(dx=2), at(dx=3), at(dy=1), at(dy=2), at(dy=3), at(dc=1)]
    peers += [at(dz=d) for d in (1, -1, 2, -2, 3, -3, 5, -5)]
    barrier = pltpu.get_barrier_semaphore()
    for peer in peers:
        pl.semaphore_signal(barrier, inc=1, device_id=peer, device_id_type=MESH)

    own_q = pltpu.make_async_copy(
        queries.at[:, pl.ds(pl.multiple_of(x * 16, 16), 16)],
        q_all.at[pl.ds(pl.multiple_of(x * 32, 32), 32)],
        local.at[0],
    )
    own_q.start()

    wide[0:80] = pooled[...].astype(F32)
    for n in range(5):
        keys = wide[pl.ds(16 * n, 8, stride=2)]
        values = wide[pl.ds(16 * n + 1, 8, stride=2)]
        z_own[0, n] = jnp.concatenate([keys, values], 0).astype(BF)
    wide[128:384] = fresh[...].astype(F32)
    for h in range(4):
        for kv in range(2):
            fresh_out[h, kv] = wide[pl.ds(128 + 2 * h + kv, 32, stride=8)].astype(BF)

    pl.semaphore_wait(barrier, len(peers))

    def send(src, dst, s, r, peer):
        copy = pltpu.make_async_remote_copy(
            src_ref=src, dst_ref=dst, send_sem=s, recv_sem=r, device_id=peer, device_id_type=MESH
        )
        copy.start()
        return copy

    started = []

    def send_z(k, src, dst, dz):
        copy = send(src, dst, zs.at[k], zr.at[k], at(dz=dz))
        started.append(copy)
        return copy

    far = [send_z(0, z_own.at[0], z_far.at[1], 5), send_z(1, z_own.at[0], z_far.at[0], -5)]
    near = [
        send_z(2 + i, z_own.at[0], z_near.at[i], d) for i, d in enumerate((-1, 1, -2, 2))
    ]

    mid = [
        [parent[5 + at(dy=j)[0] - c + cc] for cc in range(2)] for j in range(4)
    ]

    def send_y(g, zone):
        lo, hi = GROUPS[g]
        slots = pl.ds(lo, hi - lo)
        for j in (2, 1, 3):
            to_y[j - 1, 0, slots] = zone[:, 0]
            for cc in range(2):
                to_y[j - 1, 1 + cc, slots] = zone[:, mid[j][cc]]
        copies = []
        for j in (2, 1, 3):
            copies.append(
                send(
                    to_y.at[j - 1, :, slots],
                    held.at[:, 4 - j, slots],
                    ys.at[g, j - 1],
                    yr.at[g, j - 1],
                    at(dy=j),
                )
            )
        held[0, 0, slots] = zone[:, 0]
        for cc in range(2):
            held[1 + cc, 0, slots] = zone[:, mid[0][cc]]
        started.extend(copies)
        return copies

    early_y = send_y(0, z_own)

    q_in = []
    for j in (2, 1, 3):
        head = pl.multiple_of(((x + j) % 4) * 16, 16)
        q_in.append(
            send(
                queries.at[:, pl.ds(head, 16)],
                q_all.at[pl.ds(pl.multiple_of(x * 32, 32), 32)],
                qs.at[j - 1],
                qr.at[j - 1],
                at(dx=j),
            )
        )
    rows_x = pl.ds(pl.multiple_of(x * 32, 32), 32)
    f_in = []
    for j in (2, 1, 3):
        for kv in range(2):
            f_in.append(
                send(
                    fresh_out.at[(x + j) % 4, kv],
                    (k1 if kv == 0 else v1).at[rows_x, pl.ds(0, 128)],
                    fs.at[j - 1, kv],
                    fr.at[j - 1, kv],
                    at(dx=j),
                )
            )
    k1[rows_x, :] = fresh_out[x, 0]
    v1[rows_x, 0:128] = fresh_out[x, 1]

    for part in range(2):
        wide[0:256] = leaf[pl.ds(part * 256, 256)].astype(F32)
        k1[128 + part * 128 : 256 + part * 128] = wide[pl.ds(0, 128, stride=2)].astype(BF)
        v1[128 + part * 128 : 256 + part * 128, 0:128] = wide[pl.ds(1, 128, stride=2)].astype(BF)
    v1[:, 128:256] = jnp.ones((384, 128), BF)
    v2[:, 128:256] = jnp.ones((896, 128), BF)
    v3[:, 128:256] = jnp.ones((1152, 128), BF)

    b1[...] = jnp.where(lax.broadcasted_iota(I32, (8, 256), 1) < leaf_len[0] * 8, 0.0, NEG)

    my_mid = parent[5 + pool]

    def used_bias(ref, lo, hi):
        count = hi - lo
        block = 4 * count * 8
        col = lax.broadcasted_iota(I32, (8, 4 * block), 1)
        part = sum((col >= block * k).astype(I32) for k in range(1, 4))
        rest = col - part * block
        dy = sum((rest >= count * 8 * k).astype(I32) for k in range(1, 4))
        slot = (rest - dy * (count * 8)) // 8
        rel = jnp.zeros_like(slot)
        for k in range(count):
            rel = jnp.where(slot == k, (z + REL[lo + k] + 16) % 16, rel)
        core = jnp.where(part % 2 == 0, c, 1 - c)
        place = rel * 8 + ((y + dy) & 3) * 2 + core
        in_root = part < 2
        first = jnp.where(in_root, owners[0], owners[my_mid])
        many = jnp.where(in_root, pages[0], pages[my_mid])
        ref[...] = jnp.where(((place - first) & 127) < many, 0.0, NEG)

    used_bias(b2, *EARLY)
    used_bias(b3, *LATE)

    for copy in near:
        copy.wait_recv()
    early_y += send_y(1, z_near)
    for copy in far:
        copy.wait_recv()
    rest = []
    for f in range(2):
        for i, d in enumerate((1, -1, 2, -2)):
            if f == 0:
                slot = {1: 0, -1: 1, 2: 2, -2: 3}[d]
            else:
                slot = {-1: 4, 1: 5, -2: 6, 2: 7}[d]
            rest.append(send_z(6 + 4 * f + i, z_far.at[f], z_rest.at[slot], d))
    rest.append(send_z(14, z_far.at[c], z_rest.at[8], 6 * c - 3))
    early_y += send_y(2, z_far)
    for copy in rest:
        copy.wait_recv()
    late_y = send_y(3, z_rest)

    def swap(k, lo, hi):
        slots = pl.ds(lo, hi - lo)
        pair = [
            send(held.at[0, :, slots], other.at[0, :, slots], cs.at[k, 0], cr.at[k, 0], at(dc=1)),
            send(held.at[2 - c, :, slots], other.at[1, :, slots], cs.at[k, 1], cr.at[k, 1], at(dc=1)),
        ]
        started.extend(pair)
        return pair

    def gather_keys(k_ref, v_ref, lo, hi):
        count = hi - lo
        size = 4 * count * 8
        slots = pl.ds(lo, count)
        parts = (held.at[0, :, slots], other.at[0, :, slots], held.at[1 + c, :, slots], other.at[1, :, slots])
        for n, ref in enumerate(parts):
            blocks = ref[...].astype(F32).reshape(4 * count, 16, 128)
            k_ref[n * size : (n + 1) * size] = blocks[:, 0:8].reshape(size, 128).astype(BF)
            v_ref[n * size : (n + 1) * size, 0:128] = blocks[:, 8:16].reshape(size, 128).astype(BF)

    for copy in early_y:
        copy.wait_recv()
    early_c = swap(0, *EARLY)

    scale = (128 ** -0.5) * 1.4426950408889634

    def chunk_of(step):
        return (x + step) % 4

    own_q.wait()
    for copy in q_in + f_in:
        copy.wait_recv()

    def phase1(step, _):
        part = chunk_of(step)
        rows = pl.ds(pl.multiple_of(part * 512, 512), 512)
        q = q_all[pl.ds(pl.multiple_of(part * 32, 32), 32)].reshape(512, 128)
        s_new = dot_t(q, k1[0:128])
        row = part * 32 + lax.broadcasted_iota(I32, (512, 128), 0) // 16
        s_new = jnp.where(lax.broadcasted_iota(I32, (512, 128), 1) <= row, s_new, NEG)
        s_leaf = dot_t(q, k1[128:384]) + b1[0:1]
        m = jnp.maximum(jnp.max(s_new, 1, keepdims=True), jnp.max(s_leaf, 1, keepdims=True))
        p_new = jnp.exp2((s_new - m) * scale).astype(BF)
        p_leaf = jnp.exp2((s_leaf - m) * scale).astype(BF)
        acc[rows] = jnp.dot(p_new, v1[0:128], preferred_element_type=F32) + jnp.dot(
            p_leaf, v1[128:384], preferred_element_type=F32
        )
        m_ref[rows] = m
        return 0

    lax.fori_loop(0, 4, phase1, 0)

    def fold(part, k_ref, v_ref, b_ref):
        rows = pl.ds(pl.multiple_of(part * 512, 512), 512)
        q = q_all[pl.ds(pl.multiple_of(part * 32, 32), 32)].reshape(512, 128)
        s = dot_t(q, k_ref[...]) + b_ref[0:1]
        old = m_ref[rows]
        m = jnp.maximum(old, jnp.max(s, 1, keepdims=True))
        p = jnp.exp2((s - m) * scale).astype(BF)
        total = acc[rows] * jnp.exp2((old - m) * scale) + jnp.dot(
            p, v_ref[...], preferred_element_type=F32
        )
        return m, total

    for copy in early_c:
        copy.wait_recv()
    gather_keys(k2, v2, *EARLY)

    def phase2(step, _):
        part = chunk_of(step)
        rows = pl.ds(pl.multiple_of(part * 512, 512), 512)
        m, total = fold(part, k2, v2, b2)
        m_ref[rows] = m
        acc[rows] = total
        return 0

    lax.fori_loop(0, 4, phase2, 0)

    for copy in late_y:
        copy.wait_recv()
    late_c = swap(1, *LATE)
    for copy in late_c:
        copy.wait_recv()
    gather_keys(k3, v3, *LATE)

    heads = pl.ds(pl.multiple_of(x * 16, 16), 16)
    results = []
    for j in (2, 1, 3, 0):
        part = (x + j) % 4
        _, total = fold(part, k3, v3, b3)
        tile = (total[:, 0:128] / total[:, 128:256]).astype(BF)
        span = pl.ds(pl.multiple_of(part * 32, 32), 32)
        o_all[span] = tile.reshape(32, 16, 128)
        if j:
            results.append(
                send(o_all.at[span], out.at[:, heads], os.at[j - 1], orr.at[j - 1], at(dx=j))
            )
        else:
            mine = pltpu.make_async_copy(o_all.at[span], out.at[:, heads], local.at[1])
            mine.start()
    mine.wait()
    for copy in started + q_in + f_in:
        copy.wait_send()
    for copy in results:
        copy.wait()


def per_device(queries, fresh, pooled, leaf, parent, pages, owners, leaf_len):
    vmem = pl.BlockSpec(memory_space=pltpu.VMEM)
    smem = pl.BlockSpec(memory_space=pltpu.SMEM)
    dma = pltpu.SemaphoreType.DMA

    def zone(n):
        return pltpu.VMEM((n, 5, 16, 128), BF)

    return pl.pallas_call(
        kernel,
        out_shape=jax.ShapeDtypeStruct((32, 64, 128), BF),
        in_specs=[smem] * 4 + [pl.BlockSpec(memory_space=pl.ANY), vmem, vmem, vmem],
        out_specs=pl.BlockSpec(memory_space=pl.ANY),
        scratch_shapes=[
            pltpu.VMEM((128, 16, 128), BF),
            pltpu.VMEM((384, 128), BF),
            pltpu.VMEM((384, 256), BF),
            pltpu.VMEM((896, 128), BF),
            pltpu.VMEM((896, 256), BF),
            pltpu.VMEM((1152, 128), BF),
            pltpu.VMEM((1152, 256), BF),
            pltpu.VMEM((8, 256), F32),
            pltpu.VMEM((8, 896), F32),
            pltpu.VMEM((8, 1152), F32),
            pltpu.VMEM((384, 128), F32),
            pltpu.VMEM((4, 2, 32, 128), BF),
            zone(1),
            zone(4),
            zone(2),
            zone(9),
            pltpu.VMEM((3, 3, 16, 16, 128), BF),
            pltpu.VMEM((3, 4, 16, 16, 128), BF),
            pltpu.VMEM((2, 4, 16, 16, 128), BF),
            pltpu.VMEM((2048, 1), F32),
            pltpu.VMEM((2048, 256), F32),
            pltpu.VMEM((128, 16, 128), BF),
            dma((15,)),
            dma((15,)),
            dma((4, 3)),
            dma((4, 3)),
            dma((2, 2)),
            dma((2, 2)),
            dma((3,)),
            dma((3,)),
            dma((3, 2)),
            dma((3, 2)),
            dma((3,)),
            dma((3,)),
            dma((2,)),
        ],
        compiler_params=pltpu.CompilerParams(
            collective_id=0, has_side_effects=True, vmem_limit_bytes=56 << 20
        ),
    )(
        parent,
        pages,
        owners,
        leaf_len,
        queries,
        fresh.reshape(256, 128),
        pooled.reshape(80, 128),
        leaf.reshape(512, 128),
    )


def solution(mesh):
    return jax.shard_map(
        per_device,
        mesh=mesh,
        in_specs=(
            P(("pool", "tp"), None, None),
            P(("pool", "tp"), None, None, None),
            P(None, "pool", None, "tp", None, None),
            P("pool", None, "tp", None, None),
            P(),
            P(),
            P(),
            P("pool"),
        ),
        out_specs=P(("pool", "tp"), None, None),
        check_vma=False,
    )
```

```python
import jax
import jax.numpy as jnp
from jax import lax
from jax.experimental import pallas as pl
from jax.experimental.pallas import tpu as pltpu
from jax.sharding import PartitionSpec as P

MESH = pl.DeviceIdType.MESH
BF, F32, I32 = jnp.bfloat16, jnp.float32, jnp.int32
NEG = -1e30
ROWS_A, ROWS_B = 256,256

REL = (0, 1, -1, 3, -3, 4, -2, 2, -4, 6, -6, 7, -5, 5, -7, 8)
STEP = (0, -1, 1)
GROUPS = ((0, 1, 3), (3, 2, 9), (9, 2, 16))


def dot_t(a, b):
    return lax.dot_general(a, b, (((1,), (1,)), ((), ())), preferred_element_type=F32)


def kernel(
    parent_in, pages_in, owners_in, leaf_len_in, queries, fresh_in, pooled_in, leaf_in, out,
    parent, pages, owners, leaf_len, fresh, pooled, leaf,
    q_all, k1, v1, k3, v3, b1, b3, wide, fresh_out,
    z_own, z_mid, z_far, ready, ready8, held, other, m_ref, acc, o_all,
    zs, zr, ys, yr, es, er, cs, cr, qs, qr, fs, fr, os, orr, local,
):
    pool, x = lax.axis_index("pool"), lax.axis_index("tp")
    z, y, c = pool // 8, (pool // 2) % 4, pool % 2

    def at(dz=0, dy=0, dc=0, dx=0):
        place = ((z + dz + 16) % 16) * 8 + ((y + dy) % 4) * 2 + (c + dc) % 2
        return (place, (x + dx) % 4)

    targets = [(t, j) for j in (2, 1, 3, 0) for t in (1, 2, 0) if t or j]
    peers = [at(dz=3), at(dz=-3)] + [at(dz=STEP[t], dy=j) for t, j in targets]
    peers += [at(dx=1), at(dx=2), at(dx=3), at(dc=1)]
    barrier = pltpu.get_barrier_semaphore()
    for peer in peers:
        pl.semaphore_signal(barrier, inc=1, device_id=peer, device_id_type=MESH)

    def fetch(k, src, dst):
        copy = pltpu.make_async_copy(src, dst, local.at[k])
        copy.start()
        return copy

    get_pooled = fetch(0, pooled_in, pooled)
    get_fresh = fetch(1, fresh_in, fresh)
    scalars = [
        fetch(2, parent_in, parent),
        fetch(3, pages_in, pages),
        fetch(4, owners_in, owners),
        fetch(5, leaf_len_in, leaf_len),
    ]
    get_leaf = fetch(6, leaf_in, leaf)
    rows_x = pl.ds(pl.multiple_of(x * 32, 32), 32)
    heads = pl.ds(pl.multiple_of(x * 16, 16), 16)
    get_q = fetch(7, queries.at[:, heads], q_all.at[rows_x])

    get_pooled.wait()
    wide[0:80] = pooled[...].astype(F32)
    for n in range(5):
        keys = wide[pl.ds(16 * n, 8, stride=2)]
        values = wide[pl.ds(16 * n + 1, 8, stride=2)]
        z_own[0, n] = jnp.concatenate([keys, values], 0).astype(BF)

    def mids_at(dz, dy):
        first = at(dz=dz, dy=dy)[0] - c
        return [parent[5 + first], parent[6 + first]]

    pl.semaphore_wait(barrier, len(peers))

    started = []

    def send(src, dst, s, r, peer):
        copy = pltpu.make_async_remote_copy(
            src_ref=src, dst_ref=dst, send_sem=s, recv_sem=r, device_id=peer, device_id_type=MESH
        )
        copy.start()
        started.append(copy)
        return copy

    def send_z(k, src, dst, dz):
        return send(src, dst, zs.at[k], zr.at[k], at(dz=dz))

    threes = [
        send_z(0, z_own.at[0], z_mid.at[0], -3),
        send_z(1, z_own.at[0], z_mid.at[1], 3),
    ]

    q_in = []
    for j in (2, 1, 3):
        head = pl.multiple_of(((x + j) % 4) * 16, 16)
        q_in.append(
            send(queries.at[:, pl.ds(head, 16)], q_all.at[rows_x], qs.at[j - 1], qr.at[j - 1], at(dx=j))
        )

    def spread(g, zone):
        lo, n, _ = GROUPS[g]
        sets = pl.ds((0, 1, 3)[g], n)
        copies = []
        for t, j in targets:
            ready[t, j, 0, sets] = zone[:, 0]
            for cc in range(2):
                ready[t, j, 1 + cc, sets] = zone[:, mid[t][j][cc]]
            copies.append(
                send(
                    ready.at[t, j, :, sets],
                    held.at[:, (4 - j) % 4, pl.ds(lo + n * t, n)],
                    ys.at[g, t, j],
                    yr.at[g, t, j],
                    at(dz=STEP[t], dy=j),
                )
            )
        held[0, 0, lo : lo + n] = zone[:, 0]
        for cc in range(2):
            held[1 + cc, 0, lo : lo + n] = zone[:, mid[0][0][cc]]
        return copies

    for copy in scalars:
        copy.wait()
    mid = [[mids_at(STEP[t], j) for j in range(4)] for t in range(3)]
    first_in = spread(0, z_own)

    get_fresh.wait()
    wide[128:384] = fresh[...].astype(F32)
    for h in range(4):
        for kv in range(2):
            fresh_out[h, kv] = wide[pl.ds(128 + 2 * h + kv, 32, stride=8)].astype(BF)
    for j in (2, 1, 3):
        for kv in range(2):
            q_in.append(
                send(
                    fresh_out.at[(x + j) % 4, kv],
                    (k1 if kv == 0 else v1).at[rows_x, pl.ds(0, 128)],
                    fs.at[j - 1, kv],
                    fr.at[j - 1, kv],
                    at(dx=j),
                )
            )
    k1[rows_x, :] = fresh_out[x, 0]
    v1[rows_x, 0:128] = fresh_out[x, 1]

    get_leaf.wait()
    for part in range(2):
        wide[0:256] = leaf[pl.ds(part * 256, 256)].astype(F32)
        k1[128 + part * 128 : 256 + part * 128] = wide[pl.ds(0, 128, stride=2)].astype(BF)
        v1[128 + part * 128 : 256 + part * 128, 0:128] = wide[pl.ds(1, 128, stride=2)].astype(BF)
    v1[:, 128:256] = jnp.ones((1536, 128), BF)
    v3[:, 128:256] = jnp.ones((896, 128), BF)

    my_mid = parent[5 + pool]

    def used_bias(ref, col0, lo, hi):
        count = hi - lo
        block = 4 * count * 8
        col = lax.broadcasted_iota(I32, (8, 4 * block), 1)
        part = sum((col >= block * k).astype(I32) for k in range(1, 4))
        rest = col - part * block
        dy = sum((rest >= count * 8 * k).astype(I32) for k in range(1, 4))
        slot = (rest - dy * (count * 8)) // 8
        rel = jnp.zeros_like(slot)
        for k in range(count):
            rel = jnp.where(slot == k, (z + REL[lo + k] + 16) % 16, rel)
        core = jnp.where(part < 2, c, 1 - c)
        place = rel * 8 + ((y + dy) & 3) * 2 + core
        in_root = part % 2 == 0
        first = jnp.where(in_root, owners[0], owners[my_mid])
        many = jnp.where(in_root, pages[0], pages[my_mid])
        ref[:, col0 : col0 + 4 * block] = jnp.where(((place - first) & 127) < many, 0.0, NEG)

    b1[:, 0:256] = jnp.where(lax.broadcasted_iota(I32, (8, 256), 1) < leaf_len[0] * 8, 0.0, NEG)
    used_bias(b1, 256, 0, 3)

    for copy in threes:
        copy.wait_recv()
    sixes = [send_z(2, z_mid.at[0], z_far.at[0], -3), send_z(3, z_mid.at[1], z_far.at[1], 3)]
    second_in = spread(1, z_mid)

    used_bias(b1, 640, 3, 9)
    used_bias(b3, 0, 9, 16)

    def swap(g):
        slots = pl.ds(GROUPS[g][0], GROUPS[g][2] - GROUPS[g][0])
        return [
            send(held.at[0, :, slots], other.at[0, :, slots], cs.at[g, 0], cr.at[g, 0], at(dc=1)),
            send(held.at[2 - c, :, slots], other.at[1, :, slots], cs.at[g, 1], cr.at[g, 1], at(dc=1)),
        ]

    def gather_keys(k_ref, v_ref, row0, g, halves=(0, 1)):
        count = GROUPS[g][2] - GROUPS[g][0]
        size = 4 * count * 8
        slots = pl.ds(GROUPS[g][0], count)
        parts = (held.at[0, :, slots], held.at[1 + c, :, slots], other.at[0, :, slots], other.at[1, :, slots])
        for half in halves:
            for n in (2 * half, 2 * half + 1):
                blocks = parts[n][...].astype(F32).reshape(4 * count, 16, 128)
                to = slice(row0 + n * size, row0 + (n + 1) * size)
                k_ref[to] = blocks[:, 0:8].reshape(size, 128).astype(BF)
                v_ref[to, 0:128] = blocks[:, 8:16].reshape(size, 128).astype(BF)

    for copy in first_in:
        copy.wait_recv()
    first_swap = swap(0)

    for copy in sixes:
        copy.wait_recv()
    third_in = spread(2, z_far)
    for j in (2, 1, 3, 0):
        eight = mids_at(4 * c - 2, j)
        ready8[j, 0] = z_far[c, 0]
        for cc in range(2):
            ready8[j, 1 + cc] = z_far[c, eight[cc]]
        third_in.append(
            send(
                ready8.at[j],
                held.at[:, (4 - j) % 4, 15],
                es.at[j],
                er.at[j],
                at(dz=4 * c - 2, dy=j),
            )
        )

    for copy in second_in:
        copy.wait_recv()
    second_swap = swap(1)
    for copy in first_swap:
        copy.wait_recv()
    gather_keys(k1, v1, 384, 0)
    gather_keys(k1, v1, 768, 1, (0,))

    scale = (128 ** -0.5) * 1.4426950408889634

    def chunk(part, size):
        rows = pl.ds(pl.multiple_of(part * size, size), size)
        tokens = pl.ds(pl.multiple_of(part * (size // 16), size // 16), size // 16)
        return rows, tokens, q_all[tokens].reshape(size, 128)

    def start(part):
        rows, _, q = chunk(part, ROWS_A)
        s_new = dot_t(q, k1[0:128])
        row = part * (ROWS_A // 16) + lax.broadcasted_iota(I32, (ROWS_A, 128), 0) // 16
        s_new = jnp.where(lax.broadcasted_iota(I32, (ROWS_A, 128), 1) <= row, s_new, NEG)
        s_old = dot_t(q, k1[128:1536]) + b1[0:1]
        m = jnp.maximum(jnp.max(s_new, 1, keepdims=True), jnp.max(s_old, 1, keepdims=True))
        p_new = jnp.exp2((s_new - m) * scale).astype(BF)
        p_old = jnp.exp2((s_old - m) * scale).astype(BF)
        acc[rows] = jnp.dot(p_new, v1[0:128], preferred_element_type=F32) + jnp.dot(
            p_old, v1[128:1536], preferred_element_type=F32
        )
        m_ref[rows] = m

    get_q.wait()
    for copy in q_in:
        copy.wait_recv()
    for copy in second_swap:
        copy.wait_recv()
    gather_keys(k1, v1, 768, 1, (1,))
    for part in range(2048 // ROWS_A):
        if part == (2048 // ROWS_A) * 3 // 4:
            for copy in third_in:
                copy.wait_recv()
            third_swap = swap(2)
        start(part)
    gather_keys(k3, v3, 0, 2, (0,))
    for copy in third_swap:
        copy.wait_recv()
    gather_keys(k3, v3, 0, 2, (1,))

    results = []
    pieces = 512 // ROWS_B
    for j in (2, 1, 3, 0):
        for piece in range(pieces):
            rows, tokens, q = chunk((x + j) % 4 * pieces + piece, ROWS_B)
            s = dot_t(q, k3[...]) + b3[0:1]
            old = m_ref[rows]
            m = jnp.maximum(old, jnp.max(s, 1, keepdims=True))
            p = jnp.exp2((s - m) * scale).astype(BF)
            total = acc[rows] * jnp.exp2((old - m) * scale) + jnp.dot(
                p, v3[...], preferred_element_type=F32
            )
            tile = (total[:, 0:128] / total[:, 128:256]).astype(BF)
            o_all[tokens] = tile.reshape(ROWS_B // 16, 16, 128)
            there = out.at[pl.ds(piece * (ROWS_B // 16), ROWS_B // 16), heads]
            if j:
                results.append(
                    send(o_all.at[tokens], there, os.at[j - 1, piece], orr.at[j - 1, piece], at(dx=j))
                )
            else:
                results.append(fetch(8 + piece, o_all.at[tokens], there))
    for copy in started:
        copy.wait_send()
    for copy in results[: 3 * pieces]:
        copy.wait_recv()
    for copy in results[3 * pieces :]:
        copy.wait()


def per_device(queries, fresh, pooled, leaf, parent, pages, owners, leaf_len):
    dma = pltpu.SemaphoreType.DMA

    def zone(n):
        return pltpu.VMEM((n, 5, 16, 128), BF)

    return pl.pallas_call(
        kernel,
        out_shape=pltpu.VMEM((32, 64, 128), BF),
        in_specs=[pl.BlockSpec(memory_space=pltpu.HBM)] * 8,
        out_specs=pl.BlockSpec(memory_space=pltpu.VMEM),
        scratch_shapes=[
            pltpu.SMEM((133,), I32),
            pltpu.SMEM((5,), I32),
            pltpu.SMEM((5,), I32),
            pltpu.SMEM((1,), I32),
            pltpu.VMEM((256, 128), BF),
            pltpu.VMEM((80, 128), BF),
            pltpu.VMEM((512, 128), BF),
            pltpu.VMEM((128, 16, 128), BF),
            pltpu.VMEM((1536, 128), BF),
            pltpu.VMEM((1536, 256), BF),
            pltpu.VMEM((896, 128), BF),
            pltpu.VMEM((896, 256), BF),
            pltpu.VMEM((8, 1408), F32),
            pltpu.VMEM((8, 896), F32),
            pltpu.VMEM((384, 128), F32),
            pltpu.VMEM((4, 2, 32, 128), BF),
            zone(1),
            zone(2),
            zone(2),
            pltpu.VMEM((3, 4, 3, 5, 16, 128), BF),
            pltpu.VMEM((4, 3, 16, 128), BF),
            pltpu.VMEM((3, 4, 16, 16, 128), BF),
            pltpu.VMEM((2, 4, 16, 16, 128), BF),
            pltpu.VMEM((2048, 1), F32),
            pltpu.VMEM((2048, 256), F32),
            pltpu.VMEM((128, 16, 128), BF),
            dma((4,)),
            dma((4,)),
            dma((3, 3, 4)),
            dma((3, 3, 4)),
            dma((4,)),
            dma((4,)),
            dma((3, 2)),
            dma((3, 2)),
            dma((3,)),
            dma((3,)),
            dma((3, 2)),
            dma((3, 2)),
            dma((3, 512 // ROWS_B)),
            dma((3, 512 // ROWS_B)),
            dma((8 + 512 // ROWS_B,)),
        ],
        compiler_params=pltpu.CompilerParams(
            collective_id=0, has_side_effects=True, vmem_limit_bytes=56 << 20
        ),
    )(
        parent,
        pages,
        owners,
        leaf_len,
        queries,
        fresh.reshape(256, 128),
        pooled.reshape(80, 128),
        leaf.reshape(512, 128),
    )


def solution(mesh):
    return jax.shard_map(
        per_device,
        mesh=mesh,
        in_specs=(
            P(("pool", "tp"), None, None),
            P(("pool", "tp"), None, None, None),
            P(None, "pool", None, "tp", None, None),
            P("pool", None, "tp", None, None),
            P(),
            P(),
            P(),
            P("pool"),
        ),
        out_specs=P(("pool", "tp"), None, None),
        check_vma=False,
    )
```

```python
import jax
import jax.numpy as jnp
from jax import lax
from jax.experimental import pallas as pl
from jax.experimental.pallas import tpu as pltpu
from jax.sharding import PartitionSpec as P

MESH = pl.DeviceIdType.MESH
BF, F32, I32 = jnp.bfloat16, jnp.float32, jnp.int32
NEG = -1e30
ROWS_A, ROWS_B = 256, 256
WAIT_AT, AHEAD = 2, 2

REL = (0, 1, -1, 3, -3, 4, -2, 2, -4, 6, -6, 7, -5, 5, -7, 8)
STEP = (0, -1, 1)
GROUPS = ((0, 1, 3), (3, 2, 9), (9, 2, 16))


def dot_t(a, b):
    return lax.dot_general(a, b, (((1,), (1,)), ((), ())), preferred_element_type=F32)


def kernel(
    parent_in, pages_in, owners_in, leaf_len_in, queries, fresh_in, pooled_in, leaf_in, out,
    parent, pages, owners, leaf_len, fresh, pooled, leaf,
    q_all, k1, v1, k2, v2, k3, v3, b1, b2, b3, wide, fresh_out,
    z_own, z_mid, z_far, ready, ready8, held, other, m_ref, acc, o_all,
    zs, zr, ys, yr, es, er, cs, cr, qs, qr, fs, fr, os, orr, local,
):
    pool, x = lax.axis_index("pool"), lax.axis_index("tp")
    z, y, c = pool // 8, (pool // 2) % 4, pool % 2

    def at(dz=0, dy=0, dc=0, dx=0):
        place = ((z + dz + 16) % 16) * 8 + ((y + dy) % 4) * 2 + (c + dc) % 2
        return (place, (x + dx) % 4)

    targets = [(t, j) for j in (2, 1, 3, 0) for t in (1, 2, 0) if t or j]
    peers = [at(dz=3), at(dz=-3)]
    peers += [at(dz=STEP[t], dy=j) for t, j in targets]
    peers += [at(dx=1), at(dx=2), at(dx=3), at(dc=1)]
    barrier = pltpu.get_barrier_semaphore()
    for peer in peers:
        pl.semaphore_signal(barrier, inc=1, device_id=peer, device_id_type=MESH)

    def fetch(k, src, dst):
        copy = pltpu.make_async_copy(src, dst, local.at[k])
        copy.start()
        return copy

    get_pooled = fetch(0, pooled_in, pooled)
    get_fresh = fetch(1, fresh_in, fresh)
    scalars = [
        fetch(2, parent_in, parent),
        fetch(3, pages_in, pages),
        fetch(4, owners_in, owners),
        fetch(5, leaf_len_in, leaf_len),
    ]
    get_leaf = fetch(6, leaf_in, leaf)
    rows_x = pl.ds(pl.multiple_of(x * 32, 32), 32)
    heads = pl.ds(pl.multiple_of(x * 16, 16), 16)
    get_q = fetch(7, queries.at[:, heads], q_all.at[rows_x])

    get_pooled.wait()
    wide[0:80] = pooled[...].astype(F32)
    for n in range(5):
        keys = wide[pl.ds(16 * n, 8, stride=2)]
        values = wide[pl.ds(16 * n + 1, 8, stride=2)]
        z_own[0, n] = jnp.concatenate([keys, values], 0).astype(BF)

    def mids_at(dz, dy):
        return [parent[5 + at(dz=dz, dy=dy, dc=k)[0]] for k in (0, 1)]

    pl.semaphore_wait(barrier, len(peers))

    started = []

    def send(src, dst, s, r, peer):
        copy = pltpu.make_async_remote_copy(
            src_ref=src, dst_ref=dst, send_sem=s, recv_sem=r, device_id=peer, device_id_type=MESH
        )
        copy.start()
        started.append(copy)
        return copy

    def send_z(k, src, dst, dz):
        return send(src, dst, zs.at[k], zr.at[k], at(dz=dz))

    threes = [
        send_z(0, z_own.at[0], z_mid.at[0], -3),
        send_z(1, z_own.at[0], z_mid.at[1], 3),
    ]

    q_in = []
    for j in (2, 1, 3):
        head = pl.multiple_of(((x + j) % 4) * 16, 16)
        q_in.append(
            send(queries.at[:, pl.ds(head, 16)], q_all.at[rows_x], qs.at[j - 1], qr.at[j - 1], at(dx=j))
        )

    def spread(g, zone):
        lo, n, _ = GROUPS[g]
        sets = pl.ds((0, 1, 3)[g], n)
        copies = {}
        for t, j in targets:
            ready[t, j, 0, sets] = zone[:, mid[t][j][0]]
            ready[t, j, 1, sets] = zone[:, 0]
            ready[t, j, 2, sets] = zone[:, mid[t][j][1]]
            copies[t, j] = send(
                ready.at[t, j, :, sets],
                held.at[:, (4 - j) % 4, pl.ds(lo + n * t, n)],
                ys.at[g, t, j],
                yr.at[g, t, j],
                at(dz=STEP[t], dy=j),
            )
        held[0, 0, lo : lo + n] = zone[:, mid[0][0][0]]
        held[1, 0, lo : lo + n] = zone[:, 0]
        held[2, 0, lo : lo + n] = zone[:, mid[0][0][1]]
        return copies

    for copy in scalars:
        copy.wait()
    mid = [[mids_at(STEP[t], j) for j in range(4)] for t in range(3)]
    first_in = spread(0, z_own)

    get_fresh.wait()
    wide[128:384] = fresh[...].astype(F32)
    for h in range(4):
        for kv in range(2):
            fresh_out[h, kv] = wide[pl.ds(128 + 2 * h + kv, 32, stride=8)].astype(BF)
    for j in (2, 1, 3):
        for kv in range(2):
            q_in.append(
                send(
                    fresh_out.at[(x + j) % 4, kv],
                    (k1 if kv == 0 else v1).at[rows_x, pl.ds(0, 128)],
                    fs.at[j - 1, kv],
                    fr.at[j - 1, kv],
                    at(dx=j),
                )
            )
    k1[rows_x, :] = fresh_out[x, 0]
    v1[rows_x, 0:128] = fresh_out[x, 1]

    get_leaf.wait()
    for part in range(2):
        wide[0:256] = leaf[pl.ds(part * 256, 256)].astype(F32)
        k1[128 + part * 128 : 256 + part * 128] = wide[pl.ds(0, 128, stride=2)].astype(BF)
        v1[128 + part * 128 : 256 + part * 128, 0:128] = wide[pl.ds(1, 128, stride=2)].astype(BF)
    v1[:, 128:256] = jnp.ones((768, 128), BF)
    v2[:, 128:256] = jnp.ones((768, 128), BF)
    v3[:, 128:256] = jnp.ones((896, 128), BF)

    my_mid = parent[5 + pool]

    def used_bias(ref, col0, lo, hi):
        count = hi - lo
        block = 4 * count * 8
        col = lax.broadcasted_iota(I32, (8, 4 * block), 1)
        part = sum((col >= block * k).astype(I32) for k in range(1, 4))
        rest = col - part * block
        dy = sum((rest >= count * 8 * k).astype(I32) for k in range(1, 4))
        slot = (rest - dy * (count * 8)) // 8
        rel = jnp.zeros_like(slot)
        for k in range(count):
            rel = jnp.where(slot == k, (z + REL[lo + k] + 16) % 16, rel)
        core = jnp.where(part < 2, c, 1 - c)
        place = rel * 8 + ((y + dy) & 3) * 2 + core
        in_root = part % 2 == 0
        first = jnp.where(in_root, owners[0], owners[my_mid])
        many = jnp.where(in_root, pages[0], pages[my_mid])
        ref[:, col0 : col0 + 4 * block] = jnp.where(((place - first) & 127) < many, 0.0, NEG)

    b1[:, 0:256] = jnp.where(lax.broadcasted_iota(I32, (8, 256), 1) < leaf_len[0] * 8, 0.0, NEG)
    used_bias(b1, 256, 0, 3)

    for copy in threes:
        copy.wait_recv()
    sixes = [send_z(2, z_mid.at[0], z_far.at[0], -3), send_z(3, z_mid.at[1], z_far.at[1], 3)]
    second_in = spread(1, z_mid)

    used_bias(b2, 0, 3, 9)
    used_bias(b3, 0, 9, 16)

    def swap(g, k, dys):
        slots = pl.ds(GROUPS[g][0], GROUPS[g][2] - GROUPS[g][0])
        return send(held.at[1:3, dys, slots], other.at[:, dys, slots], cs.at[g, k], cr.at[g, k], at(dc=1))

    def gather_keys(k_ref, v_ref, row0, g, which=(0, 1, 2, 3)):
        count = GROUPS[g][2] - GROUPS[g][0]
        size = 4 * count * 8
        slots = pl.ds(GROUPS[g][0], count)
        for n in which:
            blocks = (held[1 - n, :, slots] if n < 2 else other[n - 2, :, slots]).astype(F32)
            blocks = blocks.reshape(4 * count, 16, 128)
            to = slice(row0 + n * size, row0 + (n + 1) * size)
            k_ref[to] = blocks[:, 0:8].reshape(size, 128).astype(BF)
            v_ref[to, 0:128] = blocks[:, 8:16].reshape(size, 128).astype(BF)

    for copy in first_in.values():
        copy.wait_recv()
    first_swap = swap(0, 0, slice(0, 4))

    for copy in sixes:
        copy.wait_recv()
    third_in = spread(2, z_far)
    eight_in = {}
    for j in (2, 1, 3, 0):
        eight = mids_at(4 * c - 2, j)
        ready8[j, 0] = z_far[c, eight[0]]
        ready8[j, 1] = z_far[c, 0]
        ready8[j, 2] = z_far[c, eight[1]]
        eight_in[j] = send(
            ready8.at[j], held.at[:, (4 - j) % 4, 15], es.at[j], er.at[j], at(dz=4 * c - 2, dy=j)
        )
    first_swap.wait_recv()
    gather_keys(k1, v1, 384, 0)

    scale = (128 ** -0.5) * 1.4426950408889634

    def chunk(part, size):
        rows = pl.ds(pl.multiple_of(part * size, size), size)
        tokens = pl.ds(pl.multiple_of(part * (size // 16), size // 16), size // 16)
        return rows, tokens, q_all[tokens].reshape(size, 128)

    def start(part):
        rows, _, q = chunk(part, ROWS_A)
        s_new = dot_t(q, k1[0:128])
        row = part * (ROWS_A // 16) + lax.broadcasted_iota(I32, (ROWS_A, 128), 0) // 16
        s_new = jnp.where(lax.broadcasted_iota(I32, (ROWS_A, 128), 1) <= row, s_new, NEG)
        s_old = dot_t(q, k1[128:768]) + b1[0:1]
        m = jnp.maximum(jnp.max(s_new, 1, keepdims=True), jnp.max(s_old, 1, keepdims=True))
        p_new = jnp.exp2((s_new - m) * scale).astype(BF)
        p_old = jnp.exp2((s_old - m) * scale).astype(BF)
        acc[rows] = jnp.dot(p_new, v1[0:128], preferred_element_type=F32) + jnp.dot(
            p_old, v1[128:768], preferred_element_type=F32
        )
        m_ref[rows] = m

    def more(part):
        rows, _, q = chunk(part, ROWS_A)
        s = dot_t(q, k2[...]) + b2[0:1]
        old = m_ref[rows]
        m = jnp.maximum(old, jnp.max(s, 1, keepdims=True))
        p = jnp.exp2((s - m) * scale).astype(BF)
        acc[rows] = acc[rows] * jnp.exp2((old - m) * scale) + jnp.dot(
            p, v2[...], preferred_element_type=F32
        )
        m_ref[rows] = m

    get_q.wait()
    for copy in q_in:
        copy.wait_recv()
    count = 2048 // ROWS_A
    for part in range(count):
        if part == count // 4:
            for copy in second_in.values():
                copy.wait_recv()
            second_swap = swap(1, 0, slice(0, 4))
        start(part)
    gather_keys(k2, v2, 0, 1, (0, 1))
    second_swap.wait_recv()
    gather_keys(k2, v2, 0, 1, (2, 3))
    for part in range(count):
        if part == WAIT_AT:
            third_swap = []
            for j in (0, 1, 3, 2):
                for t in (0, 1, 2):
                    if t or j:
                        third_in[t, j].wait_recv()
                eight_in[j].wait_recv()
                third_swap.append(swap(2, j, (4 - j) % 4))
        more(part)
    gather_keys(k3, v3, 0, 2, (0, 1))

    pieces = 512 // ROWS_B
    order = [(j, piece) for j in (2, 1, 3, 0) for piece in range(pieces)]

    def scores(j, piece, span):
        _, _, q = chunk((x + j) % 4 * pieces + piece, ROWS_B)
        return dot_t(q, k3[span]) + b3[0:1, span]

    ahead = [scores(*step, slice(0, 448)) for step in order[:AHEAD]]
    for copy in third_swap:
        copy.wait_recv()
    gather_keys(k3, v3, 0, 2, (2, 3))

    results = []
    for number, (j, piece) in enumerate(order):
        rows, tokens, _ = chunk((x + j) % 4 * pieces + piece, ROWS_B)
        old = m_ref[rows]
        if number < AHEAD:
            parts = [ahead[number], scores(j, piece, slice(448, 896))]
            spans = [slice(0, 448), slice(448, 896)]
        else:
            parts, spans = [scores(j, piece, slice(0, 896))], [slice(0, 896)]
        m = old
        for s in parts:
            m = jnp.maximum(m, jnp.max(s, 1, keepdims=True))
        total = acc[rows] * jnp.exp2((old - m) * scale)
        for s, span in zip(parts, spans):
            p = jnp.exp2((s - m) * scale).astype(BF)
            total += jnp.dot(p, v3[span], preferred_element_type=F32)
        tile = (total[:, 0:128] / total[:, 128:256]).astype(BF)
        o_all[tokens] = tile.reshape(ROWS_B // 16, 16, 128)
        there = out.at[pl.ds(piece * (ROWS_B // 16), ROWS_B // 16), heads]
        if j:
            results.append(
                send(o_all.at[tokens], there, os.at[j - 1, piece], orr.at[j - 1, piece], at(dx=j))
            )
        else:
            results.append(fetch(8 + piece, o_all.at[tokens], there))
    for copy in started:
        copy.wait_send()
    for copy in results[: 3 * pieces]:
        copy.wait_recv()
    for copy in results[3 * pieces :]:
        copy.wait()


def per_device(queries, fresh, pooled, leaf, parent, pages, owners, leaf_len):
    dma = pltpu.SemaphoreType.DMA

    def zone(n):
        return pltpu.VMEM((n, 5, 16, 128), BF)

    return pl.pallas_call(
        kernel,
        out_shape=pltpu.VMEM((32, 64, 128), BF),
        in_specs=[pl.BlockSpec(memory_space=pltpu.HBM)] * 8,
        out_specs=pl.BlockSpec(memory_space=pltpu.VMEM),
        scratch_shapes=[
            pltpu.SMEM((133,), I32),
            pltpu.SMEM((5,), I32),
            pltpu.SMEM((5,), I32),
            pltpu.SMEM((1,), I32),
            pltpu.VMEM((256, 128), BF),
            pltpu.VMEM((80, 128), BF),
            pltpu.VMEM((512, 128), BF),
            pltpu.VMEM((128, 16, 128), BF),
            pltpu.VMEM((768, 128), BF),
            pltpu.VMEM((768, 256), BF),
            pltpu.VMEM((768, 128), BF),
            pltpu.VMEM((768, 256), BF),
            pltpu.VMEM((896, 128), BF),
            pltpu.VMEM((896, 256), BF),
            pltpu.VMEM((8, 640), F32),
            pltpu.VMEM((8, 768), F32),
            pltpu.VMEM((8, 896), F32),
            pltpu.VMEM((384, 128), F32),
            pltpu.VMEM((4, 2, 32, 128), BF),
            zone(1),
            zone(2),
            zone(2),
            pltpu.VMEM((3, 4, 3, 5, 16, 128), BF),
            pltpu.VMEM((4, 3, 16, 128), BF),
            pltpu.VMEM((3, 4, 16, 16, 128), BF),
            pltpu.VMEM((2, 4, 16, 16, 128), BF),
            pltpu.VMEM((2048, 1), F32),
            pltpu.VMEM((2048, 256), F32),
            pltpu.VMEM((128, 16, 128), BF),
            dma((4,)),
            dma((4,)),
            dma((3, 3, 4)),
            dma((3, 3, 4)),
            dma((4,)),
            dma((4,)),
            dma((3, 4)),
            dma((3, 4)),
            dma((3,)),
            dma((3,)),
            dma((3, 2)),
            dma((3, 2)),
            dma((3, 512 // ROWS_B)),
            dma((3, 512 // ROWS_B)),
            dma((8 + 512 // ROWS_B,)),
        ],
        compiler_params=pltpu.CompilerParams(
            collective_id=0, has_side_effects=True, vmem_limit_bytes=56 << 20
        ),
    )(
        parent,
        pages,
        owners,
        leaf_len,
        queries,
        fresh.reshape(256, 128),
        pooled.reshape(80, 128),
        leaf.reshape(512, 128),
    )


def solution(mesh):
    return jax.shard_map(
        per_device,
        mesh=mesh,
        in_specs=(
            P(("pool", "tp"), None, None),
            P(("pool", "tp"), None, None, None),
            P(None, "pool", None, "tp", None, None),
            P("pool", None, "tp", None, None),
            P(),
            P(),
            P(),
            P("pool"),
        ),
        out_specs=P(("pool", "tp"), None, None),
        check_vma=False,
    )
```

```python
import jax
import jax.numpy as jnp
from jax import lax
from jax.experimental import pallas as pl
from jax.experimental.pallas import tpu as pltpu
from jax.sharding import PartitionSpec as P

MESH = pl.DeviceIdType.MESH
BF, F32, I32 = jnp.bfloat16, jnp.float32, jnp.int32
NEG = -1e30
ROWS_A, ROWS_B = 256, 256
WAIT_AT, AHEAD = 1, 3

REL = (0, 1, -1, 3, -3, 4, -2, 2, -4, 6, -6, 7, -5, 5, -7, 8)
STEP = (0, -1, 1)
GROUPS = ((0, 1, 3), (3, 2, 9), (9, 2, 16))


def dot_t(a, b):
    return lax.dot_general(a, b, (((1,), (1,)), ((), ())), preferred_element_type=F32)


def kernel(
    parent_in, pages_in, owners_in, leaf_len_in, queries, fresh_in, pooled_in, leaf_in, out,
    parent, pages, owners, leaf_len, fresh, pooled, leaf,
    q_all, k1, v1, k2, v2, k3, v3, b1, b2, b3, wide, fresh_out,
    z_own, z_mid, z_far, ready, ready8, held, other, m_ref, acc, o_all,
    zs, zr, ys, yr, es, er, cs, cr, qs, qr, fs, fr, os, orr, local,
):
    pool, x = lax.axis_index("pool"), lax.axis_index("tp")
    z, y, c = pool // 8, (pool // 2) % 4, pool % 2

    def at(dz=0, dy=0, dc=0, dx=0):
        place = ((z + dz + 16) % 16) * 8 + ((y + dy) % 4) * 2 + (c + dc) % 2
        return (place, (x + dx) % 4)

    targets = [(t, j) for j in (2, 1, 3, 0) for t in (1, 2, 0) if t or j]
    peers = [at(dz=3), at(dz=-3)]
    peers += [at(dz=STEP[t], dy=j) for t, j in targets]
    peers += [at(dx=1), at(dx=2), at(dx=3), at(dc=1)]
    barrier = pltpu.get_barrier_semaphore()
    for peer in peers:
        pl.semaphore_signal(barrier, inc=1, device_id=peer, device_id_type=MESH)

    def fetch(k, src, dst):
        copy = pltpu.make_async_copy(src, dst, local.at[k])
        copy.start()
        return copy

    get_pooled = fetch(0, pooled_in, pooled)
    get_fresh = fetch(1, fresh_in, fresh)
    scalars = [
        fetch(2, parent_in, parent),
        fetch(3, pages_in, pages),
        fetch(4, owners_in, owners),
        fetch(5, leaf_len_in, leaf_len),
    ]
    get_leaf = fetch(6, leaf_in, leaf)
    rows_x = pl.ds(pl.multiple_of(x * 32, 32), 32)
    heads = pl.ds(pl.multiple_of(x * 16, 16), 16)
    get_q = fetch(7, queries.at[:, heads], q_all.at[rows_x])

    get_pooled.wait()
    wide[0:80] = pooled[...].astype(F32)
    for n in range(5):
        keys = wide[pl.ds(16 * n, 8, stride=2)]
        values = wide[pl.ds(16 * n + 1, 8, stride=2)]
        z_own[0, n] = jnp.concatenate([keys, values], 0).astype(BF)

    def mids_at(dz, dy):
        return [parent[5 + at(dz=dz, dy=dy, dc=k)[0]] for k in (0, 1)]

    pl.semaphore_wait(barrier, len(peers))

    started = []

    def send(src, dst, s, r, peer):
        copy = pltpu.make_async_remote_copy(
            src_ref=src, dst_ref=dst, send_sem=s, recv_sem=r, device_id=peer, device_id_type=MESH
        )
        copy.start()
        started.append(copy)
        return copy

    def send_z(k, src, dst, dz):
        return send(src, dst, zs.at[k], zr.at[k], at(dz=dz))

    threes = [
        send_z(0, z_own.at[0], z_mid.at[0], -3),
        send_z(1, z_own.at[0], z_mid.at[1], 3),
    ]

    q_in = []
    for j in (2, 1, 3):
        head = pl.multiple_of(((x + j) % 4) * 16, 16)
        q_in.append(
            send(queries.at[:, pl.ds(head, 16)], q_all.at[rows_x], qs.at[j - 1], qr.at[j - 1], at(dx=j))
        )

    def spread(g, zone):
        lo, n, _ = GROUPS[g]
        sets = pl.ds((0, 1, 3)[g], n)
        copies = {}
        for t, j in targets:
            ready[t, j, 0, sets] = zone[:, mid[t][j][0]]
            ready[t, j, 1, sets] = zone[:, 0]
            ready[t, j, 2, sets] = zone[:, mid[t][j][1]]
            copies[t, j] = send(
                ready.at[t, j, :, sets],
                held.at[:, (4 - j) % 4, pl.ds(lo + n * t, n)],
                ys.at[g, t, j],
                yr.at[g, t, j],
                at(dz=STEP[t], dy=j),
            )
        held[0, 0, lo : lo + n] = zone[:, mid[0][0][0]]
        held[1, 0, lo : lo + n] = zone[:, 0]
        held[2, 0, lo : lo + n] = zone[:, mid[0][0][1]]
        return copies

    for copy in scalars:
        copy.wait()
    mid = [[mids_at(STEP[t], j) for j in range(4)] for t in range(3)]
    first_in = spread(0, z_own)

    get_fresh.wait()
    wide[128:384] = fresh[...].astype(F32)
    for h in range(4):
        for kv in range(2):
            fresh_out[h, kv] = wide[pl.ds(128 + 2 * h + kv, 32, stride=8)].astype(BF)
    for j in (2, 1, 3):
        for kv in range(2):
            q_in.append(
                send(
                    fresh_out.at[(x + j) % 4, kv],
                    (k1 if kv == 0 else v1).at[rows_x, pl.ds(0, 128)],
                    fs.at[j - 1, kv],
                    fr.at[j - 1, kv],
                    at(dx=j),
                )
            )
    k1[rows_x, :] = fresh_out[x, 0]
    v1[rows_x, 0:128] = fresh_out[x, 1]

    for copy in threes:
        copy.wait_recv()
    sixes = [send_z(2, z_mid.at[0], z_far.at[0], -3), send_z(3, z_mid.at[1], z_far.at[1], 3)]
    second_in = spread(1, z_mid)

    get_leaf.wait()
    for part in range(2):
        wide[0:256] = leaf[pl.ds(part * 256, 256)].astype(F32)
        k1[128 + part * 128 : 256 + part * 128] = wide[pl.ds(0, 128, stride=2)].astype(BF)
        v1[128 + part * 128 : 256 + part * 128, 0:128] = wide[pl.ds(1, 128, stride=2)].astype(BF)
    v1[:, 128:256] = jnp.ones((768, 128), BF)
    v2[:, 128:256] = jnp.ones((768, 128), BF)
    v3[:, 128:256] = jnp.ones((896, 128), BF)

    my_mid = parent[5 + pool]

    def used_bias(ref, col0, lo, hi):
        count = hi - lo
        block = 4 * count * 8
        col = lax.broadcasted_iota(I32, (8, 4 * block), 1)
        part = sum((col >= block * k).astype(I32) for k in range(1, 4))
        rest = col - part * block
        dy = sum((rest >= count * 8 * k).astype(I32) for k in range(1, 4))
        slot = (rest - dy * (count * 8)) // 8
        rel = jnp.zeros_like(slot)
        for k in range(count):
            rel = jnp.where(slot == k, (z + REL[lo + k] + 16) % 16, rel)
        core = jnp.where(part < 2, c, 1 - c)
        place = rel * 8 + ((y + dy) & 3) * 2 + core
        in_root = part % 2 == 0
        first = jnp.where(in_root, owners[0], owners[my_mid])
        many = jnp.where(in_root, pages[0], pages[my_mid])
        ref[:, col0 : col0 + 4 * block] = jnp.where(((place - first) & 127) < many, 0.0, NEG)

    b1[:, 0:256] = jnp.where(lax.broadcasted_iota(I32, (8, 256), 1) < leaf_len[0] * 8, 0.0, NEG)
    used_bias(b1, 256, 0, 3)

    used_bias(b2, 0, 3, 9)
    used_bias(b3, 0, 9, 16)

    def swap(g, k, dys):
        slots = pl.ds(GROUPS[g][0], GROUPS[g][2] - GROUPS[g][0])
        return send(held.at[1:3, dys, slots], other.at[:, dys, slots], cs.at[g, k], cr.at[g, k], at(dc=1))

    def gather_keys(k_ref, v_ref, row0, g, which=(0, 1, 2, 3)):
        count = GROUPS[g][2] - GROUPS[g][0]
        size = 4 * count * 8
        slots = pl.ds(GROUPS[g][0], count)
        for n in which:
            blocks = (held[1 - n, :, slots] if n < 2 else other[n - 2, :, slots]).astype(F32)
            blocks = blocks.reshape(4 * count, 16, 128)
            to = slice(row0 + n * size, row0 + (n + 1) * size)
            k_ref[to] = blocks[:, 0:8].reshape(size, 128).astype(BF)
            v_ref[to, 0:128] = blocks[:, 8:16].reshape(size, 128).astype(BF)

    for copy in first_in.values():
        copy.wait_recv()
    first_swap = swap(0, 0, slice(0, 4))

    for copy in sixes:
        copy.wait_recv()
    third_in = spread(2, z_far)
    eight_in = {}
    for j in (2, 1, 3, 0):
        eight = mids_at(4 * c - 2, j)
        ready8[j, 0] = z_far[c, eight[0]]
        ready8[j, 1] = z_far[c, 0]
        ready8[j, 2] = z_far[c, eight[1]]
        eight_in[j] = send(
            ready8.at[j], held.at[:, (4 - j) % 4, 15], es.at[j], er.at[j], at(dz=4 * c - 2, dy=j)
        )
    first_swap.wait_recv()
    gather_keys(k1, v1, 384, 0)

    scale = (128 ** -0.5) * 1.4426950408889634

    def chunk(part, size):
        rows = pl.ds(pl.multiple_of(part * size, size), size)
        tokens = pl.ds(pl.multiple_of(part * (size // 16), size // 16), size // 16)
        return rows, tokens, q_all[tokens].reshape(size, 128)

    def start(part):
        rows, _, q = chunk(part, ROWS_A)
        s_new = dot_t(q, k1[0:128])
        row = part * (ROWS_A // 16) + lax.broadcasted_iota(I32, (ROWS_A, 128), 0) // 16
        s_new = jnp.where(lax.broadcasted_iota(I32, (ROWS_A, 128), 1) <= row, s_new, NEG)
        s_old = dot_t(q, k1[128:768]) + b1[0:1]
        m = jnp.maximum(jnp.max(s_new, 1, keepdims=True), jnp.max(s_old, 1, keepdims=True))
        p_new = jnp.exp2((s_new - m) * scale).astype(BF)
        p_old = jnp.exp2((s_old - m) * scale).astype(BF)
        acc[rows] = jnp.dot(p_new, v1[0:128], preferred_element_type=F32) + jnp.dot(
            p_old, v1[128:768], preferred_element_type=F32
        )
        m_ref[rows] = m

    def more(part):
        rows, _, q = chunk(part, ROWS_A)
        s = dot_t(q, k2[...]) + b2[0:1]
        old = m_ref[rows]
        m = jnp.maximum(old, jnp.max(s, 1, keepdims=True))
        p = jnp.exp2((s - m) * scale).astype(BF)
        acc[rows] = acc[rows] * jnp.exp2((old - m) * scale) + jnp.dot(
            p, v2[...], preferred_element_type=F32
        )
        m_ref[rows] = m

    get_q.wait()
    for copy in q_in:
        copy.wait_recv()
    count = 2048 // ROWS_A
    for part in range(count):
        if part == count // 4:
            for copy in second_in.values():
                copy.wait_recv()
            second_swap = swap(1, 0, slice(0, 4))
        start(part)
    gather_keys(k2, v2, 0, 1, (0, 1))
    second_swap.wait_recv()
    gather_keys(k2, v2, 0, 1, (2, 3))
    for part in range(count):
        if part == WAIT_AT:
            third_swap = []
            for j in (0, 1, 3, 2):
                for t in (0, 1, 2):
                    if t or j:
                        third_in[t, j].wait_recv()
                eight_in[j].wait_recv()
                third_swap.append(swap(2, j, (4 - j) % 4))
        more(part)
    gather_keys(k3, v3, 0, 2, (0, 1))

    pieces = 512 // ROWS_B
    order = [(j, piece) for j in (2, 1, 3, 0) for piece in range(pieces)]

    def scores(j, piece, span):
        _, _, q = chunk((x + j) % 4 * pieces + piece, ROWS_B)
        return dot_t(q, k3[span]) + b3[0:1, span]

    ahead = [scores(*step, slice(0, 448)) for step in order[:AHEAD]]
    for copy in third_swap:
        copy.wait_recv()
    gather_keys(k3, v3, 0, 2, (2, 3))

    results = []
    for number, (j, piece) in enumerate(order):
        rows, tokens, _ = chunk((x + j) % 4 * pieces + piece, ROWS_B)
        old = m_ref[rows]
        if number < AHEAD:
            parts = [ahead[number], scores(j, piece, slice(448, 896))]
            spans = [slice(0, 448), slice(448, 896)]
        else:
            parts, spans = [scores(j, piece, slice(0, 896))], [slice(0, 896)]
        m = old
        for s in parts:
            m = jnp.maximum(m, jnp.max(s, 1, keepdims=True))
        total = acc[rows] * jnp.exp2((old - m) * scale)
        for s, span in zip(parts, spans):
            p = jnp.exp2((s - m) * scale).astype(BF)
            total += jnp.dot(p, v3[span], preferred_element_type=F32)
        tile = (total[:, 0:128] / total[:, 128:256]).astype(BF)
        o_all[tokens] = tile.reshape(ROWS_B // 16, 16, 128)
        there = out.at[pl.ds(piece * (ROWS_B // 16), ROWS_B // 16), heads]
        if j:
            results.append(
                send(o_all.at[tokens], there, os.at[j - 1, piece], orr.at[j - 1, piece], at(dx=j))
            )
        else:
            results.append(fetch(8 + piece, o_all.at[tokens], there))
    for copy in started:
        copy.wait_send()
    for copy in results[: 3 * pieces]:
        copy.wait_recv()
    for copy in results[3 * pieces :]:
        copy.wait()


def per_device(queries, fresh, pooled, leaf, parent, pages, owners, leaf_len):
    dma = pltpu.SemaphoreType.DMA

    def zone(n):
        return pltpu.VMEM((n, 5, 16, 128), BF)

    return pl.pallas_call(
        kernel,
        out_shape=pltpu.VMEM((32, 64, 128), BF),
        in_specs=[pl.BlockSpec(memory_space=pltpu.HBM)] * 8,
        out_specs=pl.BlockSpec(memory_space=pltpu.VMEM),
        scratch_shapes=[
            pltpu.SMEM((133,), I32),
            pltpu.SMEM((5,), I32),
            pltpu.SMEM((5,), I32),
            pltpu.SMEM((1,), I32),
            pltpu.VMEM((256, 128), BF),
            pltpu.VMEM((80, 128), BF),
            pltpu.VMEM((512, 128), BF),
            pltpu.VMEM((128, 16, 128), BF),
            pltpu.VMEM((768, 128), BF),
            pltpu.VMEM((768, 256), BF),
            pltpu.VMEM((768, 128), BF),
            pltpu.VMEM((768, 256), BF),
            pltpu.VMEM((896, 128), BF),
            pltpu.VMEM((896, 256), BF),
            pltpu.VMEM((8, 640), F32),
            pltpu.VMEM((8, 768), F32),
            pltpu.VMEM((8, 896), F32),
            pltpu.VMEM((384, 128), F32),
            pltpu.VMEM((4, 2, 32, 128), BF),
            zone(1),
            zone(2),
            zone(2),
            pltpu.VMEM((3, 4, 3, 5, 16, 128), BF),
            pltpu.VMEM((4, 3, 16, 128), BF),
            pltpu.VMEM((3, 4, 16, 16, 128), BF),
            pltpu.VMEM((2, 4, 16, 16, 128), BF),
            pltpu.VMEM((2048, 1), F32),
            pltpu.VMEM((2048, 256), F32),
            pltpu.VMEM((128, 16, 128), BF),
            dma((4,)),
            dma((4,)),
            dma((3, 3, 4)),
            dma((3, 3, 4)),
            dma((4,)),
            dma((4,)),
            dma((3, 4)),
            dma((3, 4)),
            dma((3,)),
            dma((3,)),
            dma((3, 2)),
            dma((3, 2)),
            dma((3, 512 // ROWS_B)),
            dma((3, 512 // ROWS_B)),
            dma((8 + 512 // ROWS_B,)),
        ],
        compiler_params=pltpu.CompilerParams(
            collective_id=0, has_side_effects=True, vmem_limit_bytes=56 << 20
        ),
    )(
        parent,
        pages,
        owners,
        leaf_len,
        queries,
        fresh.reshape(256, 128),
        pooled.reshape(80, 128),
        leaf.reshape(512, 128),
    )


def solution(mesh):
    return jax.shard_map(
        per_device,
        mesh=mesh,
        in_specs=(
            P(("pool", "tp"), None, None),
            P(("pool", "tp"), None, None, None),
            P(None, "pool", None, "tp", None, None),
            P("pool", None, "tp", None, None),
            P(),
            P(),
            P(),
            P("pool"),
        ),
        out_specs=P(("pool", "tp"), None, None),
        check_vma=False,
    )
```
